256 devices in a mesh: row: 32 (over x, z), col: 8 (over y, core).
Axes of the slice: x: 4, y: 4, z: 8, core: 2. Of those that a mesh axis runs over, the one named last changes fastest.
Arguments:
- tokens: bfloat16 [1536, 4096], P('row', 'col'), may hold values from -6 to 6
- cotangent: bfloat16 [1536, 4096], P('row', 'col'), may hold values from -6 to 6
- gate_weight: bfloat16 [4096, 28672], P('col', 'row'), may hold values from -0.09375 to 0.09375
- up_weight: bfloat16 [4096, 28672], P('col', 'row'), may hold values from -0.09375 to 0.09375
- down_weight: bfloat16 [28672, 4096], P('row', 'col'), may hold values from -0.03125 to 0.03125
Outputs:
- output: bfloat16 [1536, 4096], P('row', 'col')
- input_grad: bfloat16 [1536, 4096], P('row', 'col')
- gate_grad: bfloat16 [4096, 28672], P('col', 'row')
- up_grad: bfloat16 [4096, 28672], P('col', 'row')
- down_grad: bfloat16 [28672, 4096], P('row', 'col')
The draws below stay inside these ranges and needn't reach their ends.
All inputs are finite; a program needn't handle non-finite values.
Results may differ from the reference program's by a relative error of at most 0.034.
Values may be sent and summed in bfloat16 or wider, within the bound.
No kernel may reach another device: no remote copies, remote signals or barrier semaphores. Data moves between devices by JAX's collectives and lax.ppermute only.
A program may use at most 64 MiB of HBM per device.

```python
import jax
import jax.numpy as jnp

D = 4096
FF = 28672
TOKENS = 1536
N_ROW = 32
N_COL = 8


def levels(key, dims, shards, low, largest):
    loudness = 1.0
    for dim, shards_of in shards:
        steps = jax.random.uniform(jax.random.fold_in(jax.random.fold_in(key, 6), dim), (shards_of,), jnp.float32, low / len(shards), largest / len(shards))
        loudness = loudness * jnp.repeat(jnp.exp(steps), dims[dim] // shards_of).reshape((-1,) + (1,) * (len(dims) - 1 - dim))
    return loudness


def normal_values(own_key, extent, scale, reach, shards=(), held_as=jnp.bfloat16):
    drawn = jax.random.normal(own_key, extent, jnp.float32) * scale
    if len(shards) > 0:
        drawn = levels(own_key, extent, shards, -0.22, 0.18) * drawn
    return jnp.clip(drawn, min=-reach, max=reach).astype(held_as)


def setup_inputs(seed: int = 0) -> dict:
    keys = jax.random.split(jax.random.key(seed), 6)
    tokens = normal_values(keys[0], (TOKENS, D), 1.0, 6.0, ((0, 32), (1, 8)))
    cotangent = normal_values(keys[1], (TOKENS, D), 1.0, 6.0, ((0, 32), (1, 8)))
    gate_weight = normal_values(keys[2], (D, FF), D ** -0.5, 0.09375, ((0, 8), (1, 32)))
    up_weight = normal_values(keys[3], (D, FF), D ** -0.5, 0.09375, ((0, 8), (1, 32)))
    down_weight = normal_values(keys[4], (FF, D), FF ** -0.5, 0.03125, ((0, 32), (1, 8)))
    return dict(tokens=tokens, cotangent=cotangent, gate_weight=gate_weight, up_weight=up_weight, down_weight=down_weight)


def blocked_product(left_side, right_side, blocks):
    width = left_side.shape[1] // blocks
    total = jnp.zeros((left_side.shape[0], right_side.shape[1]), jnp.float32)
    for index in range(blocks):
        left_block = left_side[:, index * width:(index + 1) * width]
        right_block = right_side[index * width:(index + 1) * width, :]
        term = jnp.dot(left_block, right_block, preferred_element_type=jnp.float32).astype(jnp.bfloat16)
        total = total + term.astype(jnp.float32)
    return total


def reference(tokens, cotangent, gate_weight, up_weight, down_weight):
    gate_value = blocked_product(tokens, gate_weight, N_COL)
    up_value = blocked_product(tokens, up_weight, N_COL)
    hidden = (jax.nn.silu(gate_value) * up_value).astype(jnp.bfloat16)
    output = blocked_product(hidden, down_weight, N_ROW).astype(jnp.bfloat16)
    hidden_grad = blocked_product(cotangent, down_weight.T, N_COL)
    sigmoid_gate = jax.nn.sigmoid(gate_value)
    gate_delta = (hidden_grad * up_value * sigmoid_gate * (1.0 + gate_value * (1.0 - sigmoid_gate))).astype(jnp.bfloat16)
    up_delta = (hidden_grad * jax.nn.silu(gate_value)).astype(jnp.bfloat16)
    width = FF // N_ROW
    total = jnp.zeros((tokens.shape[0], tokens.shape[1]), jnp.float32)
    for index in range(N_ROW):
        gate_block = gate_delta[:, index * width:(index + 1) * width]
        up_block = up_delta[:, index * width:(index + 1) * width]
        term = (jnp.dot(gate_block, gate_weight[:, index * width:(index + 1) * width].T, preferred_element_type=jnp.float32)
                + jnp.dot(up_block, up_weight[:, index * width:(index + 1) * width].T, preferred_element_type=jnp.float32))
        total = total + term.astype(jnp.bfloat16).astype(jnp.float32)
    input_grad = total.astype(jnp.bfloat16)
    gate_grad = jnp.dot(tokens.T, gate_delta, preferred_element_type=jnp.float32).astype(jnp.bfloat16)
    up_grad = jnp.dot(tokens.T, up_delta, preferred_element_type=jnp.float32).astype(jnp.bfloat16)
    down_grad = jnp.dot(hidden.T, cotangent, preferred_element_type=jnp.float32).astype(jnp.bfloat16)
    return output, input_grad, gate_grad, up_grad, down_grad
```

```python
import jax
import jax.numpy as jnp
from jax import lax
from jax.sharding import PartitionSpec as P

X, Z, Y, C = 4, 8, 4, 2
F32, BF16 = jnp.float32, jnp.bfloat16


def dot(left, right, left_dim, right_dim):
    return lax.dot_general(
        left, right, (((left_dim,), (right_dim,)), ((), ())), preferred_element_type=F32
    )


def from_x(value, distance):
    return lax.ppermute(
        value,
        "row",
        [(x * Z + z, (x + distance) % X * Z + z) for x in range(X) for z in range(Z)],
    )


def from_z(value, distance):
    return lax.ppermute(
        value,
        "row",
        [(x * Z + z, x * Z + (z + distance) % Z) for x in range(X) for z in range(Z)],
    )


def from_y(value, distance):
    return lax.ppermute(
        value,
        "col",
        [(y * C + c, (y + distance) % Y * C + c) for y in range(Y) for c in range(C)],
    )


def from_core(value):
    return lax.ppermute(value, "col", [(i, i ^ 1) for i in range(Y * C)])


def swap_core(blocks, core):
    return jnp.where(core == 0, blocks, blocks[:, ::-1])


def roll_y(blocks, shift):
    return lax.dynamic_slice_in_dim(jnp.concatenate([blocks, blocks], 0), shift, Y, 0)


def gather_x(block):
    parts = [block] + [from_x(block, d) for d in range(1, X)]
    parts = [p.reshape(Y, C, 48, -1) for p in parts]
    return [
        jnp.stack([p[:, k] for p in parts], 1).reshape(Y * X * 48, -1) for k in range(C)
    ]


def sum_cols(mine, other):
    pair = (mine + from_core(other.astype(BF16)).astype(F32)).astype(BF16)
    pair = pair.reshape(Y, -1, pair.shape[-1])
    total = pair[0].astype(F32)
    for k in range(1, Y):
        total = total + from_y(pair[k], k).astype(F32)
    return total


def gather_cols(share):
    mine = jnp.concatenate([share] + [from_y(share, -k) for k in range(1, Y)], 0)
    return mine, from_core(mine)


def sum_rows(mine, other, y, core):
    n = mine.shape[-1]
    whole = jnp.stack(
        [mine.astype(BF16).reshape(Y, X, 48, n), other.astype(BF16).reshape(Y, X, 48, n)], 1
    )
    total = whole[:, :, 0].astype(F32)
    for d in range(1, X):
        total = total + from_x(whole[:, :, d], -d).astype(F32)
    total = total.astype(BF16)
    total = roll_y(swap_core(total, core), (Y - y) % Y).reshape(Z, 48, n)
    out = total[0].astype(F32)
    for d in range(1, Z):
        out = out + from_z(total[d], -d).astype(F32)
    return out.astype(BF16)


def shards(tokens, cotangent, gate_weight, up_weight, down_weight):
    col = lax.axis_index("col")
    y, core = col // C, col % C
    both = jnp.concatenate([tokens, cotangent], 1)
    blocks = jnp.stack([both] + [from_z(both, d) for d in range(1, Z)], 0)
    blocks = blocks.reshape(Y, C, 48, -1)
    blocks = roll_y(swap_core(blocks, core), y).reshape(Z * 48, -1)
    n = tokens.shape[1]
    t_mine, t_other = gather_x(blocks[:, :n])
    d_mine, d_other = gather_x(blocks[:, n:])

    gate_value = sum_cols(dot(t_mine, gate_weight, 1, 0), dot(t_other, gate_weight, 1, 0))
    up_value = sum_cols(dot(t_mine, up_weight, 1, 0), dot(t_other, up_weight, 1, 0))
    hidden_grad = sum_cols(dot(d_mine, down_weight, 1, 1), dot(d_other, down_weight, 1, 1))

    sigmoid = jax.nn.sigmoid(gate_value)
    silu = gate_value * sigmoid
    h_mine, h_other = gather_cols((silu * up_value).astype(BF16))
    gate_delta = hidden_grad * up_value * sigmoid * (1.0 + gate_value * (1.0 - sigmoid))
    g_mine, g_other = gather_cols(gate_delta.astype(BF16))
    u_mine, u_other = gather_cols((hidden_grad * silu).astype(BF16))

    output = sum_rows(dot(h_mine, down_weight, 1, 0), dot(h_other, down_weight, 1, 0), y, core)
    input_grad = sum_rows(
        dot(g_mine, gate_weight, 1, 1) + dot(u_mine, up_weight, 1, 1),
        dot(g_other, gate_weight, 1, 1) + dot(u_other, up_weight, 1, 1),
        y,
        core,
    )
    gate_grad = dot(t_mine, g_mine, 0, 0) + dot(t_other, g_other, 0, 0)
    up_grad = dot(t_mine, u_mine, 0, 0) + dot(t_other, u_other, 0, 0)
    down_grad = dot(h_mine, d_mine, 0, 0) + dot(h_other, d_other, 0, 0)
    return (
        output,
        input_grad,
        gate_grad.astype(BF16),
        up_grad.astype(BF16),
        down_grad.astype(BF16),
    )


def solution(mesh):
    rows, cols = P("row", "col"), P("col", "row")
    return jax.shard_map(
        shards,
        mesh=mesh,
        in_specs=(rows, rows, cols, cols, rows),
        out_specs=(rows, rows, cols, cols, rows),
        check_vma=False,
    )
```

```python
import jax
import jax.numpy as jnp
from jax import lax
from jax.sharding import PartitionSpec as P

X, Z, Y, C = 4, 8, 4, 2
ROWS = 48
F32, BF16 = jnp.float32, jnp.bfloat16


def dot(left, right, left_dim, right_dim):
    return lax.dot_general(
        left, right, (((left_dim,), (right_dim,)), ((), ())), preferred_element_type=F32
    )


def z_groups():
    return [
        [
            (x * Z + ((k // C + y) % Y * C + (k % C ^ c))) * Y * C + y * C + c
            for k in range(Z)
        ]
        for x in range(X)
        for y in range(Y)
        for c in range(C)
    ]


def exchange_z(blocks):
    return lax.all_to_all(
        blocks, ("row", "col"), 0, 0, axis_index_groups=z_groups(), tiled=True
    )


def from_x(value, distance):
    return lax.ppermute(
        value,
        "row",
        [(x * Z + z, (x + distance) % X * Z + z) for x in range(X) for z in range(Z)],
    )


def from_y(value, distance):
    return lax.ppermute(
        value,
        "col",
        [(y * C + c, (y + distance) % Y * C + c) for y in range(Y) for c in range(C)],
    )


def from_core(value):
    return lax.ppermute(value, "col", [(i, i ^ 1) for i in range(Y * C)])


def zero_of(other, shape):
    other = other.reshape(-1, other.shape[-1])[: shape[0], : shape[1]]
    room = [(0, want - have) for want, have in zip(shape, other.shape)]
    return jnp.pad(jnp.minimum(jnp.abs(other), 0), room)


def after(value, other):
    flat = value.reshape(-1, value.shape[-1])
    return (flat + zero_of(other, flat.shape).astype(value.dtype)).reshape(value.shape)


def copies(block):
    return jnp.broadcast_to(block[None], (Z,) + block.shape)


def whole_features(block):
    block = block.reshape(Y, C, ROWS, -1)
    return jnp.concatenate([block[:, 0], from_core(block[:, 1])], -1)


def gather_x(block):
    return [block] + [from_x(block, d) for d in range(1, X)]


def rows_of(parts):
    return jnp.stack(parts, 1).reshape(-1, parts[0].shape[-1])


def add(left, right):
    return (left.astype(F32) + right.astype(F32)).astype(BF16)


def send_far(far):
    half = far.shape[0] // 2
    return from_y(far[:half], 1), from_y(far[half:], -1)


def sum_cols(own, ahead, back, first, second):
    half = first.shape[0]
    ahead = jnp.concatenate([add(ahead[:half], first), ahead[half:]], 0)
    back = jnp.concatenate([back[:half], add(back[half:], second)], 0)
    return own.astype(F32) + from_y(ahead, 1).astype(F32) + from_y(back, -1).astype(F32)


def gather_cols(share):
    ahead, back = from_y(share, -1), from_y(share, 1)
    half = share.shape[0] // 2
    first = from_y(ahead[:half], -1)
    second = from_y(back[half:], 1)
    return [share, ahead, jnp.concatenate([first, second], 0), back]


def sum_x(value):
    value = value.reshape(Y, X, ROWS, -1)
    total = value[:, 0].astype(F32)
    for d in range(1, X):
        total = total + from_x(value[:, d], -d).astype(F32)
    return total.astype(BF16)


def shards(tokens, cotangent, gate_weight, up_weight, down_weight):
    n = gate_weight.shape[1]
    width = tokens.shape[1]
    into = jnp.concatenate([gate_weight, up_weight], 1)
    into = jnp.concatenate([into, from_core(into)], 0)
    outof = jnp.concatenate([down_weight, from_core(down_weight)], 1)

    token = whole_features(exchange_z(copies(tokens)))
    parts = gather_x(token)
    cot = whole_features(exchange_z(after(copies(cotangent), parts[1])))

    def pieces(product):
        return lax.optimization_barrier(jnp.split(product.astype(BF16), Y, 0))

    token = rows_of(parts)
    own, ahead, far, back = pieces(dot(token, into, 1, 0))
    sent = send_far(far)
    cot = rows_of(gather_x(after(cot, far)))
    values = sum_cols(own, ahead, back, *sent)

    gate_value, up_value = values[:, :n], values[:, n:]
    sigmoid = jax.nn.sigmoid(gate_value)
    silu = gate_value * sigmoid
    hidden = gather_cols((silu * up_value).astype(BF16))
    h_mine = jnp.concatenate(hidden, 0)

    own, ahead, far, back = pieces(dot(cot, outof, 1, 1))
    hidden_grad = sum_cols(own, ahead, back, *send_far(far))
    gate_delta = hidden_grad * up_value * sigmoid * (1.0 + gate_value * (1.0 - sigmoid))
    up_delta = hidden_grad * silu
    gate_delta = after(gate_delta.astype(BF16), hidden[1])
    up_delta = after(up_delta.astype(BF16), hidden[3])
    deltas = jnp.concatenate([gate_delta, up_delta], 1)
    delta = gather_cols(deltas)

    out = sum_x(dot(after(h_mine, deltas), outof, 1, 0).astype(BF16))
    delta[2] = after(delta[2], out)
    e_mine = jnp.concatenate(delta, 0)
    into_sum = sum_x(dot(e_mine, into, 1, 1).astype(BF16))

    other = from_core(jnp.concatenate([out[..., width:], into_sum[..., width:]], -1))
    own = jnp.concatenate([out[..., :width], into_sum[..., :width]], -1)
    blocks = jnp.stack([own, other], 1)
    blocks = blocks.reshape((Z,) + blocks.shape[2:])

    t_late, d_late = after(token, blocks), after(cot, blocks)
    into_grad_other = from_core(dot(t_late[:, width:], e_mine, 0, 0).astype(BF16))
    down_grad_other = from_core(dot(h_mine, d_late[:, width:], 0, 0).astype(BF16))
    into_grad = dot(t_late[:, :width], e_mine, 0, 0)
    into_grad = (into_grad + into_grad_other.astype(F32)).astype(BF16)
    down_grad = dot(h_mine, d_late[:, :width], 0, 0)
    down_grad = (down_grad + down_grad_other.astype(F32)).astype(BF16)

    blocks = exchange_z(blocks)
    blocks = after(after(blocks, into_grad), down_grad)
    result = blocks.astype(F32).sum(0).astype(BF16)
    return (
        result[:, :width],
        result[:, width:],
        into_grad[:, :n],
        into_grad[:, n:],
        down_grad,
    )


def solution(mesh):
    rows, cols = P("row", "col"), P("col", "row")
    return jax.shard_map(
        shards,
        mesh=mesh,
        in_specs=(rows, rows, cols, cols, rows),
        out_specs=(rows, rows, cols, cols, rows),
        check_vma=False,
    )
```

```python
import jax
import jax.numpy as jnp
from jax import lax
from jax.sharding import PartitionSpec as P

X, Z, Y, C = 4, 8, 4, 2
ROWS = 48
F32, BF16 = jnp.float32, jnp.bfloat16


def dot(left, right, left_dim, right_dim):
    return lax.dot_general(
        left, right, (((left_dim,), (right_dim,)), ((), ())), preferred_element_type=F32
    )


def z_groups():
    return [
        [
            (x * Z + ((k // C + y) % Y * C + (k % C ^ c))) * Y * C + y * C + c
            for k in range(Z)
        ]
        for x in range(X)
        for y in range(Y)
        for c in range(C)
    ]


def exchange_z(blocks):
    return lax.all_to_all(
        blocks, ("row", "col"), 0, 0, axis_index_groups=z_groups(), tiled=True
    )


def from_x(value, distance):
    return lax.ppermute(
        value,
        "row",
        [(x * Z + z, (x + distance) % X * Z + z) for x in range(X) for z in range(Z)],
    )


def from_y(value, distance):
    return lax.ppermute(
        value,
        "col",
        [(y * C + c, (y + distance) % Y * C + c) for y in range(Y) for c in range(C)],
    )


def from_core(value):
    return lax.ppermute(value, "col", [(i, i ^ 1) for i in range(Y * C)])


def zero_of(other, shape):
    other = other.reshape(-1, other.shape[-1])[: shape[0], : shape[1]]
    room = [(0, want - have) for want, have in zip(shape, other.shape)]
    return jnp.pad(jnp.minimum(jnp.abs(other), 0), room)


def after(value, other):
    flat = value.reshape(-1, value.shape[-1])
    return (flat + zero_of(other, flat.shape).astype(value.dtype)).reshape(value.shape)


def copies(block):
    return jnp.broadcast_to(block[None], (Z,) + block.shape)


def whole_features(block):
    block = block.reshape(Y, C, ROWS, -1)
    return jnp.concatenate([block[:, 0], from_core(block[:, 1])], -1)


def gather_x(block):
    return [block] + [from_x(block, d) for d in range(1, X)]


def rows_of(parts):
    return jnp.stack(parts, 1).reshape(-1, parts[0].shape[-1])


def add(left, right):
    return (left.astype(F32) + right.astype(F32)).astype(BF16)


def send_far(far):
    half = far.shape[0] // 2
    return from_y(far[:half], 1), from_y(far[half:], -1)


def sum_cols(own, ahead, back, first, second):
    half = first.shape[0]
    ahead = jnp.concatenate([add(ahead[:half], first), ahead[half:]], 0)
    back = jnp.concatenate([back[:half], add(back[half:], second)], 0)
    return own.astype(F32) + from_y(ahead, 1).astype(F32) + from_y(back, -1).astype(F32)


def gather_cols(share):
    ahead, back = from_y(share, -1), from_y(share, 1)
    half = share.shape[0] // 2
    first = from_y(ahead[:half], -1)
    second = from_y(back[half:], 1)
    return [share, ahead, jnp.concatenate([first, second], 0), back]


def sum_x(value):
    value = value.reshape(Y, X, ROWS, -1)
    total = value[:, 0].astype(F32)
    for d in range(1, X):
        total = total + from_x(value[:, d], -d).astype(F32)
    return total.astype(BF16), value[:, 1]


def shards(tokens, cotangent, gate_weight, up_weight, down_weight):
    n = gate_weight.shape[1]
    width = tokens.shape[1]
    into = jnp.concatenate([gate_weight, up_weight], 1)
    into = jnp.concatenate([into, from_core(into)], 0)
    outof = jnp.concatenate([down_weight, from_core(down_weight)], 1)

    token = whole_features(exchange_z(copies(tokens)))
    parts = gather_x(token)
    cot = whole_features(exchange_z(after(copies(cotangent), parts[1])))

    def pieces(product):
        return lax.optimization_barrier(jnp.split(product.astype(BF16), Y, 0))

    token = rows_of(parts)
    own, ahead, far, back = pieces(dot(token, into, 1, 0))
    sent = send_far(far)
    cot = rows_of(gather_x(after(cot, far)))
    values = sum_cols(own, ahead, back, *sent)

    gate_value, up_value = values[:, :n], values[:, n:]
    sigmoid = jax.nn.sigmoid(gate_value)
    silu = gate_value * sigmoid
    hidden = gather_cols((silu * up_value).astype(BF16))
    h_mine = jnp.concatenate(hidden, 0)

    own, ahead, far, back = pieces(dot(cot, outof, 1, 1))
    hidden_grad = sum_cols(own, ahead, back, *send_far(far))
    gate_delta = hidden_grad * up_value * sigmoid * (1.0 + gate_value * (1.0 - sigmoid))
    up_delta = hidden_grad * silu
    gate_delta = after(gate_delta.astype(BF16), hidden[1])
    up_delta = after(up_delta.astype(BF16), hidden[3])
    deltas = jnp.concatenate([gate_delta, up_delta], 1)
    delta = gather_cols(deltas)

    out, _ = sum_x(dot(after(h_mine, deltas), outof, 1, 0).astype(BF16))
    delta[2] = after(delta[2], out)
    e_mine = jnp.concatenate(delta, 0)
    into_sum, sent = sum_x(dot(e_mine, into, 1, 1).astype(BF16))

    other = from_core(jnp.concatenate([out[..., width:], into_sum[..., width:]], -1))
    own = jnp.concatenate([out[..., :width], into_sum[..., :width]], -1)
    blocks = jnp.stack([own, other], 1)
    blocks = blocks.reshape((Z,) + blocks.shape[2:])

    t_other, d_other = after(token, sent), after(cot, sent)
    into_grad_other = from_core(dot(t_other[:, width:], e_mine, 0, 0).astype(BF16))
    down_grad_other = from_core(dot(h_mine, d_other[:, width:], 0, 0).astype(BF16))
    t_mine, d_mine = after(token, blocks), after(cot, blocks)
    into_grad = dot(t_mine[:, :width], e_mine, 0, 0)
    into_grad = (into_grad + into_grad_other.astype(F32)).astype(BF16)
    down_grad = dot(h_mine, d_mine[:, :width], 0, 0)
    down_grad = (down_grad + down_grad_other.astype(F32)).astype(BF16)

    blocks = exchange_z(blocks)
    result = blocks[0].astype(F32)
    for block in blocks[1:]:
        result = result + block.astype(F32)
    result = after(after(result, into_grad), down_grad).astype(BF16)
    return (
        result[:, :width],
        result[:, width:],
        into_grad[:, :n],
        into_grad[:, n:],
        down_grad,
    )


def solution(mesh):
    rows, cols = P("row", "col"), P("col", "row")
    return jax.shard_map(
        shards,
        mesh=mesh,
        in_specs=(rows, rows, cols, cols, rows),
        out_specs=(rows, rows, cols, cols, rows),
        check_vma=False,
    )
```

```python
import jax
import jax.numpy as jnp
from jax import lax
from jax.sharding import PartitionSpec as P

X, Z, Y, C = 4, 8, 4, 2
ROWS = 48
F32, BF16 = jnp.float32, jnp.bfloat16


def dot(left, right, left_dim, right_dim):
    return lax.dot_general(
        left, right, (((left_dim,), (right_dim,)), ((), ())), preferred_element_type=F32
    )


def z_groups():
    return [
        [
            (x * Z + ((k // C + y) % Y * C + (k % C ^ c))) * Y * C + y * C + c
            for k in range(Z)
        ]
        for x in range(X)
        for y in range(Y)
        for c in range(C)
    ]


def exchange_z(blocks):
    return lax.all_to_all(
        blocks, ("row", "col"), 0, 0, axis_index_groups=z_groups(), tiled=True
    )


def from_x(value, distance):
    return lax.ppermute(
        value,
        "row",
        [(x * Z + z, (x + distance) % X * Z + z) for x in range(X) for z in range(Z)],
    )


def from_y(value, distance):
    return lax.ppermute(
        value,
        "col",
        [(y * C + c, (y + distance) % Y * C + c) for y in range(Y) for c in range(C)],
    )


def from_core(value):
    return lax.ppermute(value, "col", [(i, i ^ 1) for i in range(Y * C)])


def zero_of(other, shape):
    other = other.reshape(-1, other.shape[-1])[: shape[0], : shape[1]]
    room = [(0, want - have) for want, have in zip(shape, other.shape)]
    return jnp.pad(jnp.minimum(jnp.abs(other), 0), room)


def after(value, other):
    flat = value.reshape(-1, value.shape[-1])
    return (flat + zero_of(other, flat.shape).astype(value.dtype)).reshape(value.shape)


def copies(block):
    return jnp.broadcast_to(block[None], (Z,) + block.shape)


def whole_features(block):
    block = block.reshape(Y, C, ROWS, -1)
    return jnp.concatenate([block[:, 0], from_core(block[:, 1])], -1)


def gather_x(block):
    return [block] + [from_x(block, d) for d in range(1, X)]


def rows_of(parts):
    return jnp.stack(parts, 1).reshape(-1, parts[0].shape[-1])


def add(left, right):
    return (left.astype(F32) + right.astype(F32)).astype(BF16)


def send_far(far):
    half = far.shape[0] // 2
    return from_y(far[:half], 1), from_y(far[half:], -1)


def sum_cols(own, ahead, back, first, second):
    half = first.shape[0]
    ahead = jnp.concatenate([add(ahead[:half], first), ahead[half:]], 0)
    back = jnp.concatenate([back[:half], add(back[half:], second)], 0)
    return own.astype(F32) + from_y(ahead, 1).astype(F32) + from_y(back, -1).astype(F32)


def gather_cols(share):
    ahead, back = from_y(share, -1), from_y(share, 1)
    half = share.shape[0] // 2
    first = from_y(ahead[:half], -1)
    second = from_y(back[half:], 1)
    return [share, ahead, jnp.concatenate([first, second], 0), back]


def sum_x(value):
    value = value.reshape(Y, X, ROWS, -1)
    total = value[:, 0].astype(F32)
    for d in range(1, X):
        total = total + from_x(value[:, d], -d).astype(F32)
    return total.astype(BF16), value[:, 1]


def shards(tokens, cotangent, gate_weight, up_weight, down_weight):
    n = gate_weight.shape[1]
    width = tokens.shape[1]
    into = jnp.concatenate([gate_weight, up_weight], 1)
    into = jnp.concatenate([into, from_core(into)], 0)
    outof = jnp.concatenate([down_weight, from_core(down_weight)], 1)
    outof = lax.optimization_barrier(outof)

    token = whole_features(exchange_z(copies(tokens)))
    parts = gather_x(token)
    cot = whole_features(exchange_z(after(copies(cotangent), parts[1])))

    def pieces(product):
        return lax.optimization_barrier(jnp.split(product.astype(BF16), Y, 0))

    token = rows_of(parts)
    own, ahead, far, back = pieces(dot(token, into, 1, 0))
    sent = send_far(far)
    cot = rows_of(gather_x(after(cot, far)))
    values = sum_cols(own, ahead, back, *sent)

    gate_value, up_value = values[:, :n], values[:, n:]
    sigmoid = jax.nn.sigmoid(gate_value)
    silu = gate_value * sigmoid
    hidden = gather_cols((silu * up_value).astype(BF16))
    h_mine = jnp.concatenate(hidden, 0)

    own, ahead, far, back = pieces(dot(cot, outof, 1, 1))
    hidden_grad = sum_cols(own, ahead, back, *send_far(far))
    gate_delta = hidden_grad * up_value * sigmoid * (1.0 + gate_value * (1.0 - sigmoid))
    up_delta = hidden_grad * silu
    gate_delta = after(gate_delta.astype(BF16), hidden[1])
    up_delta = after(up_delta.astype(BF16), hidden[3])
    deltas = jnp.concatenate([gate_delta, up_delta], 1)
    delta = gather_cols(deltas)

    out, _ = sum_x(dot(after(h_mine, deltas), outof, 1, 0).astype(BF16))
    delta[2] = after(delta[2], out)
    e_mine = jnp.concatenate(delta, 0)
    into_sum, sent = sum_x(dot(e_mine, into, 1, 1).astype(BF16))

    out_other = from_core(out[..., width:])
    other = jnp.concatenate([out_other, from_core(into_sum[..., width:])], -1)
    own = jnp.concatenate([out[..., :width], into_sum[..., :width]], -1)
    blocks = jnp.stack([own, other], 1)
    blocks = blocks.reshape((Z,) + blocks.shape[2:])

    t_other, d_other = after(token, sent), after(cot, sent)
    into_grad_other = from_core(dot(t_other[:, width:], e_mine, 0, 0).astype(BF16))
    down_grad_other = from_core(dot(h_mine, d_other[:, width:], 0, 0).astype(BF16))
    t_mine, d_mine = after(token, blocks), after(cot, blocks)
    into_grad = dot(t_mine[:, :width], e_mine, 0, 0)
    into_grad = (into_grad + into_grad_other.astype(F32)).astype(BF16)
    down_grad = dot(h_mine, d_mine[:, :width], 0, 0)
    down_grad = (down_grad + down_grad_other.astype(F32)).astype(BF16)

    blocks = exchange_z(blocks)
    result = blocks[0].astype(F32)
    for block in blocks[1:]:
        result = result + block.astype(F32)
    result = after(after(result, into_grad), down_grad).astype(BF16)
    return (
        result[:, :width],
        result[:, width:],
        into_grad[:, :n],
        into_grad[:, n:],
        down_grad,
    )


def solution(mesh):
    rows, cols = P("row", "col"), P("col", "row")
    return jax.shard_map(
        shards,
        mesh=mesh,
        in_specs=(rows, rows, cols, cols, rows),
        out_specs=(rows, rows, cols, cols, rows),
        check_vma=False,
    )
```
